128 devices in a mesh: seq: 8 (over y_hi, x), rep: 16 (over y_lo, z, core).
Axes of the slice: x: 4, y: 4 (y_hi: 2, y_lo: 2; y = y_hi * 2 + y_lo), z: 4, core: 2. Of those that a mesh axis runs over, the one named last changes fastest.
Arguments:
- inputs: bfloat16 [16, 8192, 768], P('rep', 'seq'), may hold values from -6 to 6
- trunk_grad: bfloat16 [16, 4096, 1536], P('rep', None, 'seq'), may hold values from -6 to 6
- weights: bfloat16 [5, 768, 1536], P(None, 'rep', 'seq'), may hold values from -0.09375 to 0.09375
Outputs:
- input_grad: bfloat16 [16, 8192, 768], P('rep', 'seq')
- weight_grad: float32 [5, 768, 1536], P(None, 'rep', 'seq')
The draws below stay inside these ranges and needn't reach their ends.
All inputs are finite; a program needn't handle non-finite values.
Results may differ from the reference program's by a relative error of at most 0.0027.
Values may be sent and summed in bfloat16 or wider, within the bound.
A program may use at most 192 MiB of HBM per device.

```python
import jax
import jax.numpy as jnp
from jax import lax

CIN = 768
COUT = 1536
KW = 5
FINE = 8192
COARSE = 4096
SEQS = 16
NF = 131072


def shard_levels(stream_key, dims, split, smallest, top_value):
    def one(dim, shards_of):
        steps = jax.random.uniform(jax.random.fold_in(jax.random.fold_in(stream_key, 6), dim), (shards_of,), jnp.float32, smallest / len(split), top_value / len(split))
        return jnp.repeat(jnp.exp(steps), dims[dim] // shards_of).reshape((-1,) + (1,) * (len(dims) - dim - 1))

    gain = one(*split[0])
    for cut in split[1:]:
        gain = gain * one(*cut)
    return gain


def gaussian(own_key, shape, deviation, most, cuts=(), kind=jnp.bfloat16):
    result = jax.random.normal(own_key, shape, jnp.float32) * deviation
    if len(cuts) > 0:
        result = shard_levels(own_key, shape, cuts, -0.22, 0.18) * result
    return jnp.clip(result, min=-most, max=most).astype(kind)


def setup_inputs(seed: int = 0) -> dict:
    splits = jax.random.split(jax.random.key(seed), 4)
    return {
        "inputs": gaussian(splits[0], (SEQS, FINE, CIN), 1.0, 6.0, ((0, 16), (1, 8))),
        "trunk_grad": gaussian(splits[1], (SEQS, COARSE, COUT), 1.0, 6.0, ((0, 16), (2, 8))),
        "weights": gaussian(splits[2], (KW, CIN, COUT), (KW * CIN) ** -0.5, 0.09375, ((1, 16), (2, 8))),
    }


def one_sequence(weights, total, pair):
    seq_in, seq_grad = pair
    grad_up = jnp.repeat(seq_grad.astype(jnp.float32) * 0.5, 2, axis=0).astype(jnp.bfloat16)
    inputs_f = seq_in.astype(jnp.float32)
    act_vals, back = jax.vjp(jax.nn.gelu, inputs_f)
    slope = back(jnp.ones_like(inputs_f))[0]
    act = act_vals.astype(jnp.bfloat16)
    padded = jnp.pad(grad_up, ((2, 2), (0, 0)))
    act_grad = jnp.zeros((FINE, CIN), jnp.float32)
    terms = []
    for k in range(KW):
        shifted = padded[4 - k:4 - k + FINE]
        act_grad = act_grad + jnp.dot(shifted, weights[k].T, preferred_element_type=jnp.float32)
        terms.append(lax.dot_general(act, shifted, (((0,), (0,)), ((), ())), preferred_element_type=jnp.float32))
    input_grad = (act_grad * slope + grad_up[:, :CIN].astype(jnp.float32)).astype(jnp.bfloat16)
    return (total + jnp.stack(terms), input_grad)

def reference(inputs, trunk_grad, weights):

    def step_fn(total, pair):
        return one_sequence(weights, total, pair)
    start = jnp.zeros((KW, CIN, COUT), jnp.float32)
    total, input_grad = lax.scan(step_fn, start, (inputs, trunk_grad))
    weight_grad = total * float(NF) ** (-0.5)
    return (input_grad, weight_grad)
```

```python
import functools

import jax
import jax.numpy as jnp
from jax import lax
from jax.experimental import pallas as pl
from jax.experimental.pallas import tpu as pltpu
from jax.sharding import PartitionSpec as P

MESH = pl.DeviceIdType.MESH
BF = jnp.bfloat16
F32 = jnp.float32

CIN, COUT, KW = 768, 1536, 5
HALF = CIN // 2
ROWS = 512
HALO = 16
EXT = ROWS + 2 * HALO
BLK = 48
PIECE = 368
PARTS = ((0, 128), (128, 128), (256, 112))


def nt(left, right):
    return lax.dot_general(
        left, right, (((1,), (1,)), ((), ())), preferred_element_type=F32
    )


def nn(left, right):
    return jnp.dot(left, right, preferred_element_type=F32)


def low_lanes(shape):
    return lax.broadcasted_iota(jnp.int32, shape, len(shape) - 1) < 64


def swap(value):
    return pltpu.roll(value, 64, 1)


def pack(direct, other):
    low = low_lanes(direct.shape)
    rolled = swap(other)
    return jnp.where(low, direct, rolled), jnp.where(low, rolled, direct)


def unpack(first, second):
    low = low_lanes(first.shape)
    return jnp.where(low, first, second), swap(jnp.where(low, second, first))


def channel_of(column, core):
    other = column >= HALF
    col = jnp.where(other, column - HALF, column)
    block = jnp.zeros_like(col)
    for t in range(1, 8):
        block = block + (col >= t * BLK).astype(jnp.int32)
    parity = jnp.where(other, 1 - core, core)
    return (2 * block + parity) * BLK + (col - block * BLK)


def kernel(
    x_hbm, g_hbm, w_hbm, dx_ref, wg_ref,
    xin, gin, win, smain, stail, gbuf, tails, gs, shifty, perm, sel,
    xh, xo, xr, xr2, do, eot, slope, wa, wfull, wg, r1a, r1b, r1c,
    s1a, s1b, s1c, r2a, r2b, r2c, s2a, s2b, s2c, r3a, r3b, r3c, fin, p1, p3,
    lsem, ssem, rsem,
):
    s = lax.axis_index("seq")
    r = lax.axis_index("rep")
    x, yhi = lax.rem(s, 4), s // 4
    ylo, z, core = r // 8, lax.rem(r // 2, 4), lax.rem(r, 2)
    y = yhi * 2 + ylo
    odd = lax.rem(x, 2) == 1

    def dev(px, py, pz, pc):
        return ((py // 2) * 4 + px, (lax.rem(py, 2) * 4 + pz) * 2 + pc)

    def at(axis, d):
        c = {"x": x, "y": y, "z": z}
        c[axis] = lax.rem(c[axis] + d, 4)
        return dev(c["x"], c["y"], c["z"], core), c[axis]

    other_core = dev(x, y, z, 1 - core)

    load_x = pltpu.make_async_copy(x_hbm.at[0], xin, lsem.at[0])
    load_g = pltpu.make_async_copy(g_hbm.at[0], gin, lsem.at[1])
    load_w = pltpu.make_async_copy(w_hbm, win, lsem.at[2])
    load_w.start()
    load_g.start()
    load_x.start()

    barrier = pltpu.get_barrier_semaphore()
    friends = [at(axis, d)[0] for axis in "xyz" for d in (1, 2, 3)]
    friends += [dev(lax.rem(x + d, 4), lax.rem(y + 2, 4), z, core) for d in (1, 2, 3)]
    friends.append(other_core)
    for friend in friends:
        pl.semaphore_signal(barrier, inc=1, device_id=friend, device_id_type=MESH)

    count = [0]

    def remote(src, dst, device):
        i = count[0]
        count[0] += 1
        return pltpu.make_async_remote_copy(
            src_ref=src, dst_ref=dst, send_sem=ssem.at[i], recv_sem=rsem.at[i],
            device_id=device, device_id_type=MESH,
        )

    load_w.wait()
    mine = wa.at[x, y, z]

    def tail_of(tap):
        return win[tap, :, 128:192].astype(F32)

    def placed(first, second):
        both = jnp.concatenate([first, second], axis=1)
        return jnp.where(odd, swap(both), both).astype(BF)

    for tap in range(KW):
        mine[tap * BLK : (tap + 1) * BLK, :] = win[tap, :, :128]
    mine[240:288, :] = placed(tail_of(0), tail_of(1))
    mine[288:336, :] = placed(tail_of(2), tail_of(3))
    last = tail_of(4)
    mine[336:368, :] = placed(
        last[:32], jnp.concatenate([last[32:], jnp.zeros((16, 64), F32)], axis=0)
    )

    pl.semaphore_wait(barrier, len(friends))

    ranges = [pl.ds(start, size) for start, size in PARTS]
    ga, gb, gc = ranges

    def spread(axis, ref):
        copies = [remote(ref, ref, at(axis, d)[0]) for d in (1, 2, 3)]
        for c in copies:
            c.start()
        return copies

    gather1 = (
        spread("x", wa.at[x, y, z, ga])
        + spread("y", wa.at[x, y, z, gb])
        + spread("z", wa.at[x, y, z, gc])
    )

    load_g.wait()
    smain[0:HALO, :] = jnp.zeros((HALO, 128), BF)
    smain[HALO + 4096 : 2 * HALO + 4096, :] = jnp.zeros((HALO, 128), BF)

    @pl.loop(0, 8)
    def _(part):
        rows = pl.ds(pl.multiple_of(part * 512, 512), 512)
        smain[pl.ds(pl.multiple_of(part * 512 + HALO, 16), 512), :] = gin[rows, :128]

    def tail_rows(start):
        return gin[pl.ds(pl.multiple_of(start, 16), 256), 128:192].astype(F32)

    @pl.loop(0, 8)
    def _(part):
        base = part * 512
        before = gin[
            pl.ds(pl.multiple_of(jnp.maximum(base - HALO, 0), 16), HALO), 128:192
        ].astype(F32)
        before = jnp.where(part == 0, 0.0, before)
        after = gin[
            pl.ds(pl.multiple_of(jnp.minimum(base + 512, 4096 - HALO), 16), HALO), 128:192
        ].astype(F32)
        after = jnp.where(part == 7, 0.0, after)
        top = jnp.concatenate([before, tail_rows(base)], axis=0)
        bottom = jnp.concatenate([tail_rows(base + 256), after], axis=0)
        stail[part] = placed(top, bottom)

    scatter_g = []
    for dy in (0, 1):
        for dx_ in range(4):
            if dx_ == 0 and dy == 0:
                continue
            px, phi = lax.rem(x + dx_, 4), lax.rem(yhi + dy, 2)
            ps = phi * 4 + px
            target = dev(px, phi * 2 + ylo, z, core)
            rows = pl.ds(pl.multiple_of(ps * 512, 512), EXT)
            scatter_g.append(remote(smain.at[rows], gbuf.at[0, s], target))
            scatter_g.append(remote(stail.at[ps], tails.at[s], target))
    for c in scatter_g:
        c.start()
    gbuf[0, s] = smain[pl.ds(pl.multiple_of(s * 512, 512), EXT), :]
    tails[s] = stail[s]

    row_i = lax.broadcasted_iota(jnp.int32, (CIN, CIN), 0)
    col_i = lax.broadcasted_iota(jnp.int32, (CIN, CIN), 1)
    perm[...] = jnp.where(row_i == channel_of(col_i, core), 1.0, 0.0).astype(BF)

    load_x.wait()

    @pl.loop(0, 4)
    def _(part):
        rows = pl.ds(pl.multiple_of(part * 256, 256), 256)
        ordered = nn(xin[rows, :], perm[...])
        for c in range(3):
            xh[0, c, rows, :] = ordered[:, c * 128 : (c + 1) * 128]
        xo[rows, :] = ordered[:, HALF:].astype(BF)

    swap_x = remote(xo, xr, other_core)
    swap_x.start()

    for c in gather1:
        c.wait()
    gather2 = (
        spread("y", wa.at[:, y, z, ga])
        + spread("z", wa.at[x, :, z, gb])
        + spread("x", wa.at[x, y, :, gc])
    )

    def activate(q, part):
        for phase in (0, 1):
            for c in range(3):
                v = xh[q, c, pl.ds(part * 256 + phase, 128, stride=2), :]
                sq = v * v
                u = 0.7978845608028654 * (v + 0.044715 * (sq * v))
                t = jnp.tanh(u)
                half = 0.5 * (1.0 + t)
                act = (v * half).astype(BF)
                grad = half + 0.5 * v * (1.0 - t * t) * (
                    0.7978845608028654 * (1.0 + 3.0 * 0.044715 * sq)
                )
                cols = pl.ds(pl.multiple_of(q * 512 + part * 128, 128), 128)
                lo = phase * HALF + c * 128
                eot[lo : lo + 128, cols] = act.astype(F32).T.astype(BF)
                slope[phase, c, cols, :] = grad

    @pl.loop(0, 4)
    def _(part):
        activate(0, part)

    for c in gather2:
        c.wait()
    gather3 = (
        spread("z", wa.at[:, :, z, ga])
        + spread("x", wa.at[x, :, :, gb])
        + spread("y", wa.at[:, y, :, gc])
    )

    swap_x.wait()

    @pl.loop(0, 4)
    def _(part):
        rows = pl.ds(pl.multiple_of(part * 256, 256), 256)
        for c in range(3):
            xh[1, c, rows, :] = xr[rows, c * 128 : (c + 1) * 128].astype(F32)

    @pl.loop(0, 4)
    def _(part):
        activate(1, part)

    row_s = lax.broadcasted_iota(jnp.int32, (CIN, HALF), 0)
    col_s = lax.broadcasted_iota(jnp.int32, (CIN, HALF), 1)
    is_tail = row_s >= 512
    tail_s = (row_s - 512) // 64
    natural = jnp.where(
        is_tail,
        tail_s * 192 + 128 + (row_s - 512 - tail_s * 64),
        (row_s // 128) * 192 + lax.rem(row_s, 128),
    )
    sel[...] = jnp.where(natural == channel_of(col_s, core), 1.0, 0.0).astype(BF)

    for c in scatter_g:
        c.wait()

    @pl.loop(0, 4)
    def _(m):
        top, bottom = unpack(tails[2 * m].astype(F32), tails[2 * m + 1].astype(F32))
        gbuf[0, 8 + m, 0 : EXT // 2, :] = top.astype(BF)
        gbuf[0, 8 + m, EXT // 2 : EXT, :] = bottom.astype(BF)

    swap_g = remote(gbuf.at[0], gbuf.at[1], other_core)
    swap_g.start()

    def shifted(q):
        rows = slice(q * ROWS, (q + 1) * ROWS)

        @pl.loop(0, 12)
        def _(t):
            cols = pl.ds(pl.multiple_of(t * 128, 128), 128)
            shifty[...] = gbuf[q, t].astype(F32)
            for j in (0, 1, 2):
                gs[j, rows, cols] = shifty[HALO - 1 + j : HALO - 1 + j + ROWS, :].astype(BF)

    shifted(0)
    swap_g.wait()
    shifted(1)

    scale = 0.5 * float(16 * 8192) ** (-0.5)

    def grads(start):
        cols = pl.ds(pl.multiple_of(start, 128), 256)
        sums = [nn(eot[...], gs[j, :, cols]) * scale for j in (0, 1, 2)]
        a = [v[:HALF] for v in sums]
        b = [v[HALF:] for v in sums]
        return (a[2] + b[2], a[1] + b[2], a[1] + b[1], a[0] + b[1], a[0] + b[0])

    @pl.loop(0, 4)
    def _(n):
        taps = grads(n * 256)
        for half in (0, 1):
            px = lax.rem(n, 2) * 2 + half
            for b in range(8):
                target = wg.at[px, (n // 2) * 2 + b // 4, b % 4]
                for k in range(KW):
                    target[k * BLK : (k + 1) * BLK, :] = taps[k][
                        b * BLK : (b + 1) * BLK, half * 128 : (half + 1) * 128
                    ].astype(BF)

    @pl.loop(0, 2)
    def _(n):
        taps = grads(1024 + n * 256)
        for m in (0, 1):
            lanes = slice(m * 128, (m + 1) * 128)
            for b in range(8):
                rows = slice(b * BLK, (b + 1) * BLK)
                v = [tap[rows, lanes] for tap in taps]
                first = wg.at[m * 2, n * 2 + b // 4, b % 4]
                second = wg.at[m * 2 + 1, n * 2 + b // 4, b % 4]
                for lo, hi, one, two in (
                    (240, 288, v[0], v[1]),
                    (288, 336, v[2], v[3]),
                    (
                        336, 368, v[4][:32],
                        jnp.concatenate([v[4][32:], jnp.zeros((16, 128), F32)], axis=0),
                    ),
                ):
                    left, right = pack(one, two)
                    first[lo:hi, :] = left.astype(BF)
                    second[lo:hi, :] = right.astype(BF)

    def send_sums(axis, source, slots):
        copies = []
        for d in (1, 2, 3):
            device, c = at(axis, d)
            copies.append(remote(source(c), slots.at[d - 1], device))
        for c in copies:
            c.start()
        return copies

    reduce1 = (
        send_sums("z", lambda c: wg.at[:, :, c, ga], r1a)
        + send_sums("x", lambda c: wg.at[c, :, :, gb], r1b)
        + send_sums("y", lambda c: wg.at[:, c, :, gc], r1c)
    )

    for c in gather3:
        c.wait()

    @pl.loop(0, 8)
    def _(b):
        bhi, blo = b // 4, lax.rem(b, 4)
        base = b * BLK
        rows = pl.ds(pl.multiple_of(base, 16), BLK)
        for t in range(8):
            source = wa.at[t % 4, (t // 4) * 2 + bhi, blo]
            for k in range(KW):
                wfull[k, rows, t * 128 : (t + 1) * 128] = source[k * BLK : (k + 1) * BLK, :]
        for m in range(4):
            lanes = slice(1024 + m * 128, 1152 + m * 128)
            first = wa.at[(2 * m) % 4, (m // 2) * 2 + bhi, blo]
            second = wa.at[(2 * m + 1) % 4, (m // 2) * 2 + bhi, blo]
            for lo, k in ((240, 0), (288, 2)):
                one, two = unpack(
                    first[lo : lo + BLK, :].astype(F32), second[lo : lo + BLK, :].astype(F32)
                )
                wfull[k, rows, lanes] = one.astype(BF)
                wfull[k + 1, rows, lanes] = two.astype(BF)
            one, two = unpack(first[336:368, :].astype(F32), second[336:368, :].astype(F32))
            wfull[4, pl.ds(pl.multiple_of(base, 16), 32), lanes] = one.astype(BF)
            wfull[4, pl.ds(pl.multiple_of(base + 32, 16), 16), lanes] = two[:16].astype(BF)

    def inputs_back(q):
        @pl.loop(0, 2)
        def _(part):
            rows = pl.ds(pl.multiple_of(q * 512 + part * 256, 256), 256)
            middle = gs[1, rows, :]
            shared = (
                nt(gs[2, rows, :], wfull[0])
                + nt(middle, wfull[2])
                + nt(gs[0, rows, :], wfull[4])
            )
            p1[...] = nt(gs[1, rows, :], wfull[1])
            p3[...] = nt(gs[1, rows, :], wfull[3])
            after = nt(gs[2, rows, :], wfull[1])
            before = nt(gs[0, rows, :], wfull[3])
            skip = nn(
                jnp.concatenate([middle[:, :512], middle[:, 1024:1280]], axis=1), sel[...]
            )
            even = shared + p1[...] + before
            odd_ = shared + after + p3[...]
            for phase, value in ((0, even), (1, odd_)):
                for c in range(3):
                    lanes = slice(c * 128, (c + 1) * 128)
                    out = 0.5 * (value[:, lanes] * slope[phase, c, rows, :] + skip[:, lanes])
                    xh[q, c, pl.ds(part * 512 + phase, 256, stride=2), :] = out

    inputs_back(1)

    @pl.loop(0, 4)
    def _(part):
        rows = pl.ds(pl.multiple_of(part * 256, 256), 256)
        for c in range(3):
            do[rows, c * 128 : (c + 1) * 128] = xh[1, c, rows, :].astype(BF)

    swap_d = remote(do, xr2, other_core)
    swap_d.start()
    inputs_back(0)

    for c in reduce1:
        c.wait()

    def add_up(own, slots, out, lead):
        @pl.loop(0, lead[0])
        def _(i):
            for j in range(lead[1]):
                total = own(i, j).astype(F32)
                for d in range(3):
                    total = total + slots[d, i, j].astype(F32)
                out[i, j] = total.astype(out.dtype)

    add_up(lambda i, j: wg[i, j, z, ga, :], r1a, s1a, (4, 4))
    add_up(lambda i, j: wg[x, i, j, gb, :], r1b, s1b, (4, 4))
    add_up(lambda i, j: wg[i, y, j, gc, :], r1c, s1c, (4, 4))
    reduce2 = (
        send_sums("y", lambda c: s1a.at[:, c], r2a)
        + send_sums("z", lambda c: s1b.at[:, c], r2b)
        + send_sums("x", lambda c: s1c.at[c], r2c)
    )

    swap_d.wait()

    @pl.loop(0, 4)
    def _(part):
        rows = pl.ds(pl.multiple_of(part * 256, 256), 256)
        both = jnp.concatenate(
            [xh[0, c, rows, :].astype(BF) for c in range(3)] + [xr2[rows, :]], axis=1
        )
        dx_ref[0, rows, :] = nt(both, perm[...]).astype(BF)

    for c in reduce2:
        c.wait()

    def add_up2(own, slots, out):
        for i in range(4):
            total = own(i).astype(F32)
            for d in range(3):
                total = total + slots[d, i].astype(F32)
            out[i] = total

    add_up2(lambda i: s1a[i, y], r2a, s2a)
    add_up2(lambda i: s1b[i, z], r2b, s2b)
    add_up2(lambda i: s1c[x, i], r2c, s2c)
    reduce3 = (
        send_sums("x", lambda c: s2a.at[c], r3a)
        + send_sums("y", lambda c: s2b.at[c], r3b)
        + send_sums("z", lambda c: s2c.at[c], r3c)
    )
    for c in reduce3:
        c.wait()
    for (start, size), own, slots in zip(
        PARTS, (s2a[x], s2b[y], s2c[z]), (r3a, r3b, r3c)
    ):
        fin[start : start + size, :] = own + slots[0] + slots[1] + slots[2]
    for k in range(KW):
        wg_ref[k, :, 0:128] = fin[k * BLK : (k + 1) * BLK, :]

    def unplaced(lo, hi):
        value = fin[lo:hi, :]
        value = jnp.where(odd, swap(value), value)
        return value[:, :64], swap(value)[:, :64]

    for lo, k in ((240, 0), (288, 2)):
        one, two = unplaced(lo, lo + BLK)
        wg_ref[k, :, 128:192] = one
        wg_ref[k + 1, :, 128:192] = two
    one, two = unplaced(336, 368)
    wg_ref[4, 0:32, 128:192] = one
    wg_ref[4, 32:48, 128:192] = two[:16]


def on_device(inputs, trunk_grad, weights):
    sizes = [size for _, size in PARTS]
    vm = pltpu.VMEM
    scratch = [
        vm((1024, CIN), BF), vm((4096, 192), BF), vm((KW, BLK, 192), BF),
        vm((4096 + 2 * HALO, 128), BF), vm((8, EXT // 2, 128), BF),
        vm((2, 12, EXT, 128), BF), vm((8, EXT // 2, 128), BF),
        vm((3, 2 * ROWS, COUT), BF), vm((EXT, 128), F32),
        vm((CIN, CIN), BF), vm((CIN, HALF), BF),
        vm((2, 3, 1024, 128), F32), vm((1024, HALF), BF), vm((1024, HALF), BF),
        vm((1024, HALF), BF), vm((1024, HALF), BF),
        vm((CIN, 1024), BF), vm((2, 3, 1024, 128), F32),
        vm((4, 4, 4, PIECE, 128), BF), vm((KW, HALF, COUT), BF),
        vm((4, 4, 4, PIECE, 128), BF),
    ]
    scratch += [vm((3, 4, 4, n, 128), BF) for n in sizes]
    scratch += [vm((4, 4, n, 128), BF) for n in sizes]
    scratch += [vm((3, 4, n, 128), BF) for n in sizes]
    scratch += [vm((4, n, 128), F32) for n in sizes]
    scratch += [vm((3, n, 128), F32) for n in sizes]
    scratch += [vm((PIECE, 128), F32), vm((256, HALF), F32), vm((256, HALF), F32)]
    copies = 27 + 14 + 3 + 27
    scratch += [
        pltpu.SemaphoreType.DMA((3,)),
        pltpu.SemaphoreType.DMA((copies,)),
        pltpu.SemaphoreType.DMA((copies,)),
    ]
    return pl.pallas_call(
        kernel,
        out_shape=(
            jax.ShapeDtypeStruct((1, 1024, CIN), BF),
            jax.ShapeDtypeStruct((KW, BLK, 192), F32),
        ),
        in_specs=[pl.BlockSpec(memory_space=pl.ANY)] * 3,
        out_specs=(pl.BlockSpec(memory_space=pltpu.VMEM),) * 2,
        scratch_shapes=scratch,
        compiler_params=pltpu.CompilerParams(
            collective_id=0, has_side_effects=True, vmem_limit_bytes=63 * 1024 * 1024
        ),
        name="block_backward",
    )(inputs, trunk_grad, weights)


def solution(mesh):
    in_specs = (P("rep", "seq", None), P("rep", None, "seq"), P(None, "rep", "seq"))
    out_specs = (P("rep", "seq", None), P(None, "rep", "seq"))
    return jax.shard_map(
        on_device, mesh=mesh, in_specs=in_specs, out_specs=out_specs, check_vma=False
    )
```

```python
import functools

import jax
import jax.numpy as jnp
from jax import lax
from jax.experimental import pallas as pl
from jax.experimental.pallas import tpu as pltpu
from jax.sharding import PartitionSpec as P

MESH = pl.DeviceIdType.MESH
BF = jnp.bfloat16
F32 = jnp.float32

CIN, COUT, KW = 768, 1536, 5
HALF = CIN // 2
ROWS = 512
HALO = 16
EXT = ROWS + 2 * HALO
BLK = 48
PIECE = 368
GATHER = ((0, 128), (128, 128), (256, 112))
REDUCE = (((0, 80), (80, 80), (160, 80)), ((240, 48), (288, 48), (336, 32)))
TILE = 288


def nt(left, right):
    return lax.dot_general(
        left, right, (((1,), (1,)), ((), ())), preferred_element_type=F32
    )


def nn(left, right):
    return jnp.dot(left, right, preferred_element_type=F32)


def low_lanes(shape):
    return lax.broadcasted_iota(jnp.int32, shape, len(shape) - 1) < 64


def swap(value):
    return pltpu.roll(value, 64, 1)


def pack(direct, other):
    low = low_lanes(direct.shape)
    rolled = swap(other)
    return jnp.where(low, direct, rolled), jnp.where(low, rolled, direct)


def unpack(first, second):
    low = low_lanes(first.shape)
    return jnp.where(low, first, second), swap(jnp.where(low, second, first))


def channel_of(column, core):
    other = column >= HALF
    col = jnp.where(other, column - HALF, column)
    block = jnp.zeros_like(col)
    for t in range(1, 8):
        block = block + (col >= t * BLK).astype(jnp.int32)
    parity = jnp.where(other, 1 - core, core)
    return (2 * block + parity) * BLK + (col - block * BLK)


def kernel(
    x_hbm, g_hbm, w_hbm, dx_ref, wg_ref,
    xin, gin, win, gpad, stail, grad, tails, perm, sel,
    xh, xo, xr, xr2, do, et, eot, slope, wa, wfull, wg, prod, fin, *rest,
):
    def four(n):
        return [[rest[n * 6 + g * 3 + p] for p in range(3)] for g in range(2)]

    r1, s1, r2, s2, r3 = [four(n) for n in range(5)]
    lsem, ssem, rsem = rest[30:]
    s = lax.axis_index("seq")
    r = lax.axis_index("rep")
    x, yhi = lax.rem(s, 4), s // 4
    ylo, z, core = r // 8, lax.rem(r // 2, 4), lax.rem(r, 2)
    y = yhi * 2 + ylo
    odd = lax.rem(x, 2) == 1

    def dev(px, py, pz, pc):
        return ((py // 2) * 4 + px, (lax.rem(py, 2) * 4 + pz) * 2 + pc)

    def at(axis, d):
        c = {"x": x, "y": y, "z": z}
        c[axis] = lax.rem(c[axis] + d, 4)
        return dev(c["x"], c["y"], c["z"], core), c[axis]

    other_core = dev(x, y, z, 1 - core)

    load_x = pltpu.make_async_copy(x_hbm.at[0], xin, lsem.at[0])
    load_g = pltpu.make_async_copy(g_hbm.at[0], gin, lsem.at[1])
    load_w = pltpu.make_async_copy(w_hbm, win, lsem.at[2])
    load_w.start()
    load_g.start()
    load_x.start()

    barrier = pltpu.get_barrier_semaphore()
    friends = [at(axis, d)[0] for axis in "xyz" for d in (1, 2, 3)]
    friends += [dev(lax.rem(x + d, 4), lax.rem(y + 2, 4), z, core) for d in (1, 2, 3)]
    friends.append(other_core)
    for friend in friends:
        pl.semaphore_signal(barrier, inc=1, device_id=friend, device_id_type=MESH)

    count = [0]

    def remote(src, dst, device):
        i = count[0]
        count[0] += 1
        return pltpu.make_async_remote_copy(
            src_ref=src, dst_ref=dst, send_sem=ssem.at[i], recv_sem=rsem.at[i],
            device_id=device, device_id_type=MESH,
        )

    load_w.wait()
    mine = wa.at[x, y, z]

    def tail_of(tap):
        return win[tap, :, 128:192].astype(F32)

    def placed(first, second):
        both = jnp.concatenate([first, second], axis=1)
        return jnp.where(odd, swap(both), both).astype(BF)

    for tap in range(KW):
        mine[tap * BLK : (tap + 1) * BLK, :] = win[tap, :, :128]
    mine[240:288, :] = placed(tail_of(0), tail_of(1))
    mine[288:336, :] = placed(tail_of(2), tail_of(3))
    last = tail_of(4)
    mine[336:368, :] = placed(
        last[:32], jnp.concatenate([last[32:], jnp.zeros((16, 64), F32)], axis=0)
    )

    ga, gb, gc = [pl.ds(start, size) for start, size in GATHER]
    ahead = 1 - 2 * core

    def at_ahead(axis, n):
        return at(axis, n * ahead + 4)

    class Line:
        def __init__(self, axis, block):
            self.axis, self.block = axis, block
            self.onward, _ = at_ahead(axis, 1)
            back, self.before = at_ahead(axis, -1)
            own = block({"x": x, "y": y, "z": z}[axis])
            self.first = remote(own, own, self.onward)
            self.second = remote(own, own, back)
            self.first.start()
            self.second.start()

        def relay(self):
            self.first.wait_recv()
            block = self.block(self.before)
            self.third = remote(block, block, self.onward)
            self.third.start()

        def finish(self):
            self.first.wait_send()
            self.second.wait()
            self.third.wait()

    def relay(lines):
        for line in lines:
            line.relay()

    def finish(lines):
        for line in lines:
            line.finish()

    def spread(axis, block):
        copies = [remote(block, block, at(axis, d)[0]) for d in (1, 2, 3)]
        for c in copies:
            c.start()
        return copies

    def settle(copies):
        for c in copies:
            c.wait()

    load_g.wait()
    gpad[0:HALO, :] = jnp.zeros((HALO, 192), BF)
    gpad[HALO + 4096 : 2 * HALO + 4096, :] = jnp.zeros((HALO, 192), BF)

    @pl.loop(0, 8)
    def _(part):
        cols = pl.ds(pl.multiple_of(part * 512, 512), 512)
        gpad[pl.ds(pl.multiple_of(part * 512 + HALO, 16), 512), :] = gin[:, cols].T

    @pl.loop(0, 8)
    def _(part):
        def half(start):
            rows = pl.ds(pl.multiple_of(part * 512 + start, 16), EXT // 2)
            return gpad[rows, 128:192].astype(F32)

        stail[part] = placed(half(0), half(EXT // 2))

    my_lanes = pl.ds(pl.multiple_of(s * 128, 128), 128)
    grad[0, :, my_lanes] = gpad[pl.ds(pl.multiple_of(s * 512, 512), EXT), 0:128]
    tails[s] = stail[s]

    row_i = lax.broadcasted_iota(jnp.int32, (CIN, CIN), 0)
    col_i = lax.broadcasted_iota(jnp.int32, (CIN, CIN), 1)
    perm[...] = jnp.where(row_i == channel_of(col_i, core), 1.0, 0.0).astype(BF)

    pl.semaphore_wait(barrier, len(friends))


    gather1 = (
        spread("x", wa.at[x, y, z, ga])
        + spread("y", wa.at[x, y, z, gb])
        + spread("z", wa.at[x, y, z, gc])
    )

    scatter_g = []
    for dy in (0, 1):
        for dx_ in range(4):
            if dx_ == 0 and dy == 0:
                continue
            px, phi = lax.rem(x + dx_, 4), lax.rem(yhi + dy, 2)
            ps = phi * 4 + px
            target = dev(px, phi * 2 + ylo, z, core)
            rows = pl.ds(pl.multiple_of(ps * 512, 512), EXT)
            scatter_g.append(remote(gpad.at[rows, 0:128], grad.at[0, :, my_lanes], target))
            scatter_g.append(remote(stail.at[ps], tails.at[s], target))
    for c in scatter_g:
        c.start()

    load_x.wait()

    @pl.loop(0, 4)
    def _(part):
        rows = pl.ds(pl.multiple_of(part * 256, 256), 256)
        ordered = nn(xin[rows, :], perm[...])
        for c in range(3):
            xh[0, c, rows, :] = ordered[:, c * 128 : (c + 1) * 128]
        xo[rows, :] = ordered[:, HALF:].astype(BF)

    swap_x = remote(xo, xr, other_core)
    swap_x.start()

    settle(gather1)
    gather2 = (
        spread("y", wa.at[:, y, z, ga])
        + spread("z", wa.at[x, :, z, gb])
        + spread("x", wa.at[x, y, :, gc])
    )

    def activate(q, part):
        for phase in (0, 1):
            for c in range(3):
                v = xh[q, c, pl.ds(part * 256 + phase, 128, stride=2), :]
                sq = v * v
                u = 0.7978845608028654 * (v + 0.044715 * (sq * v))
                t = jnp.tanh(u)
                half = 0.5 * (1.0 + t)
                act = (v * half).astype(BF)
                deriv = half + 0.5 * v * (1.0 - t * t) * (
                    0.7978845608028654 * (1.0 + 3.0 * 0.044715 * sq)
                )
                rows = pl.ds(pl.multiple_of(q * 512 + part * 128, 128), 128)
                cols = pl.ds(pl.multiple_of(part * 128, 128), 128)
                lo = phase * HALF + c * 128
                et[lo : lo + 128, cols] = act.astype(F32).T
                slope[phase, c, rows, :] = deriv

    def shift(q):
        @pl.loop(0, 6)
        def _(n):
            rows = pl.ds(pl.multiple_of(n * 128, 128), 128)
            cols = slice(q * 512, (q + 1) * 512)
            lane = lax.broadcasted_iota(jnp.int32, (128, 512), 1)
            edge = lax.broadcasted_iota(jnp.int32, (128, 64), 1)
            v = et[rows, :]
            eot[1, rows, cols] = v.astype(BF)
            eot[0, rows, cols] = jnp.where(lane == 511, 0.0, pltpu.roll(v, 511, 1)).astype(BF)
            eot[2, rows, cols] = jnp.where(lane == 0, 0.0, pltpu.roll(v, 1, 1)).astype(BF)
            for j, here, column in ((0, q * 32 + 15, v[:, 0:1]), (2, q * 32 + 16, v[:, 511:512])):
                old = eot[j, rows, 1024:1088].astype(F32) if q else 0.0
                eot[j, rows, 1024:1088] = jnp.where(edge == here, column, old).astype(BF)

    @pl.loop(0, 2)
    def _(part):
        activate(0, part)

    settle(gather2)
    gather3 = [
        Line("z", lambda c: wa.at[:, :, c, ga]),
        Line("x", lambda c: wa.at[c, :, :, gb]),
        Line("y", lambda c: wa.at[:, c, :, gc]),
    ]

    @pl.loop(2, 4)
    def _(part):
        activate(0, part)

    shift(0)

    swap_x.wait()

    @pl.loop(0, 4)
    def _(part):
        rows = pl.ds(pl.multiple_of(part * 256, 256), 256)
        for c in range(3):
            xh[1, c, rows, :] = xr[rows, c * 128 : (c + 1) * 128].astype(F32)

    @pl.loop(0, 4)
    def _(part):
        activate(1, part)

    shift(1)

    row_s = lax.broadcasted_iota(jnp.int32, (CIN, HALF), 0)
    col_s = lax.broadcasted_iota(jnp.int32, (CIN, HALF), 1)
    is_tail = row_s >= 512
    tail_s = (row_s - 512) // 64
    natural = jnp.where(
        is_tail,
        tail_s * 192 + 128 + (row_s - 512 - tail_s * 64),
        (row_s // 128) * 192 + lax.rem(row_s, 128),
    )
    sel[...] = jnp.where(natural == channel_of(col_s, core), 1.0, 0.0).astype(BF)

    for c in scatter_g:
        c.wait()
    swap_g = remote(grad.at[0, :, 0:1024], grad.at[1, :, 0:1024], other_core)
    swap_g.start()

    for m in range(4):
        lanes = slice(1024 + m * 128, 1152 + m * 128)
        top, bottom = unpack(tails[2 * m].astype(F32), tails[2 * m + 1].astype(F32))
        grad[0, 0 : EXT // 2, lanes] = top.astype(BF)
        grad[0, EXT // 2 : EXT, lanes] = bottom.astype(BF)
    swap_t = remote(grad.at[0, :, 1024:1536], grad.at[1, :, 1024:1536], other_core)
    swap_t.start()
    swap_g.wait()
    swap_t.wait()

    scale = 0.5 * float(16 * 8192) ** (-0.5)

    def grads(start):
        cols = pl.ds(pl.multiple_of(start, 128), 256)
        right = jnp.concatenate(
            [grad[q, HALO : HALO + ROWS, cols] for q in (0, 1)]
            + [grad[q, lo : lo + HALO, cols] for q in (0, 1) for lo in (0, HALO + ROWS)],
            axis=0,
        )
        sums = [
            nn(eot[0, :, :1088], right) * scale,
            nn(eot[1, :, :1024], right[:1024]) * scale,
            nn(eot[2, :, :1088], right) * scale,
        ]
        a = [v[:HALF] for v in sums]
        b = [v[HALF:] for v in sums]
        return (a[2] + b[2], a[1] + b[2], a[1] + b[1], a[0] + b[1], a[0] + b[0])

    def main_tile(n):
        taps = grads(n * 256)
        for half in (0, 1):
            px = lax.rem(n, 2) * 2 + half
            for b in range(8):
                target = wg.at[px, (n // 2) * 2 + b // 4, b % 4]
                for k in range(KW):
                    target[k * BLK : (k + 1) * BLK, :] = taps[k][
                        b * BLK : (b + 1) * BLK, half * 128 : (half + 1) * 128
                    ].astype(BF)

    @pl.loop(0, 3)
    def _(n):
        main_tile(n)

    relay(gather3)
    main_tile(3)

    def send_sums(axis, source, slots):
        copies = []
        for d in (1, 2, 3):
            device, c = at(axis, d)
            copies.append(remote(source(c), slots.at[d - 1], device))
        for c in copies:
            c.start()
        return copies

    def reduce_first(g):
        ra, rb, rc = [pl.ds(start, size) for start, size in REDUCE[g]]
        return (
            send_sums("z", lambda c: wg.at[:, :, c, ra], r1[g][0])
            + send_sums("x", lambda c: wg.at[c, :, :, rb], r1[g][1])
            + send_sums("y", lambda c: wg.at[:, c, :, rc], r1[g][2])
        )

    def reduce_second(g, copies):
        settle(copies)
        ra, rb, rc = [pl.ds(start, size) for start, size in REDUCE[g]]
        (a1, b1, c1), (a2, b2, c2), (a3, b3, c3) = r1[g], s1[g], r2[g]
        add_up(lambda i, j: wg[i, j, z, ra, :], a1, a2)
        add_up(lambda i, j: wg[x, i, j, rb, :], b1, b2)
        add_up(lambda i, j: wg[i, y, j, rc, :], c1, c2)
        return (
            send_sums("y", lambda c: a2.at[:, c], a3)
            + send_sums("z", lambda c: b2.at[:, c], b3)
            + send_sums("x", lambda c: c2.at[c], c3)
        )

    def reduce_third(g, copies):
        settle(copies)
        (a1, b1, c1), (a2, b2, c2), (a3, b3, c3), (a4, b4, c4) = s1[g], r2[g], s2[g], r3[g]
        add_up2(lambda i: a1[i, y], a2, a3)
        add_up2(lambda i: b1[i, z], b2, b3)
        add_up2(lambda i: c1[x, i], c2, c3)
        return (
            send_sums("x", lambda c: a3.at[c], a4)
            + send_sums("y", lambda c: b3.at[c], b4)
            + send_sums("z", lambda c: c3.at[c], c4)
        )

    def reduce_last(g, copies):
        settle(copies)
        for (start, size), own, slots in zip(
            REDUCE[g], (s2[g][0][x], s2[g][1][y], s2[g][2][z]), r3[g]
        ):
            fin[start : start + size, :] = own + slots[0] + slots[1] + slots[2]

    def add_up(own, slots, out):
        @pl.loop(0, 4)
        def _(i):
            for j in range(4):
                total = own(i, j).astype(F32)
                for d in range(3):
                    total = total + slots[d, i, j].astype(F32)
                out[i, j] = total.astype(out.dtype)

    def add_up2(own, slots, out):
        for i in range(4):
            total = own(i).astype(F32)
            for d in range(3):
                total = total + slots[d, i].astype(F32)
            out[i] = total

    first0 = reduce_first(0)

    @pl.loop(0, 2)
    def _(n):
        taps = grads(1024 + n * 256)
        for m in (0, 1):
            lanes = slice(m * 128, (m + 1) * 128)
            for b in range(8):
                rows = slice(b * BLK, (b + 1) * BLK)
                v = [tap[rows, lanes] for tap in taps]
                first = wg.at[m * 2, n * 2 + b // 4, b % 4]
                second = wg.at[m * 2 + 1, n * 2 + b // 4, b % 4]
                for lo, hi, one, two in (
                    (240, 288, v[0], v[1]),
                    (288, 336, v[2], v[3]),
                    (
                        336, 368, v[4][:32],
                        jnp.concatenate([v[4][32:], jnp.zeros((16, 128), F32)], axis=0),
                    ),
                ):
                    left, right = pack(one, two)
                    first[lo:hi, :] = left.astype(BF)
                    second[lo:hi, :] = right.astype(BF)

    first1 = reduce_first(1)

    finish(gather3)

    @pl.loop(0, 8)
    def _(b):
        bhi, blo = b // 4, lax.rem(b, 4)
        base = b * BLK
        rows = pl.ds(pl.multiple_of(base, 16), BLK)
        for t in range(8):
            source = wa.at[t % 4, (t // 4) * 2 + bhi, blo]
            for k in range(KW):
                wfull[k, rows, t * 128 : (t + 1) * 128] = source[k * BLK : (k + 1) * BLK, :]
        for m in range(4):
            lanes = slice(1024 + m * 128, 1152 + m * 128)
            first = wa.at[(2 * m) % 4, (m // 2) * 2 + bhi, blo]
            second = wa.at[(2 * m + 1) % 4, (m // 2) * 2 + bhi, blo]
            for lo, k in ((240, 0), (288, 2)):
                one, two = unpack(
                    first[lo : lo + BLK, :].astype(F32), second[lo : lo + BLK, :].astype(F32)
                )
                wfull[k, rows, lanes] = one.astype(BF)
                wfull[k + 1, rows, lanes] = two.astype(BF)
            one, two = unpack(first[336:368, :].astype(F32), second[336:368, :].astype(F32))
            wfull[4, pl.ds(pl.multiple_of(base, 16), 32), lanes] = one.astype(BF)
            wfull[4, pl.ds(pl.multiple_of(base + 32, 16), 16), lanes] = two[:16].astype(BF)

    def inputs_back(q):
        @pl.loop(0, 2)
        def _(part):
            block = grad[q, pl.ds(pl.multiple_of(part * 256, 256), TILE), :]
            for n, k in enumerate((0, 1, 3, 4)):
                prod[n] = nt(block, wfull[k])
            middle = block[HALO : HALO + 256]
            skip = nn(
                jnp.concatenate([middle[:, :512], middle[:, 1024:1280]], axis=1), sel[...]
            )
            shared = nt(middle, wfull[2])
            here = slice(HALO, HALO + 256)
            after = slice(HALO + 1, HALO + 257)
            before = slice(HALO - 1, HALO + 255)
            shared = shared + prod[0, after, :] + prod[3, before, :]
            even = shared + prod[1, here, :] + prod[2, before, :]
            odd_ = shared + prod[1, after, :] + prod[2, here, :]
            rows = pl.ds(pl.multiple_of(q * 512 + part * 256, 256), 256)
            for phase, value in ((0, even), (1, odd_)):
                for c in range(3):
                    lanes = slice(c * 128, (c + 1) * 128)
                    out = 0.5 * (value[:, lanes] * slope[phase, c, rows, :] + skip[:, lanes])
                    xh[q, c, pl.ds(part * 512 + phase, 256, stride=2), :] = out

    inputs_back(1)

    @pl.loop(0, 4)
    def _(part):
        rows = pl.ds(pl.multiple_of(part * 256, 256), 256)
        for c in range(3):
            do[rows, c * 128 : (c + 1) * 128] = xh[1, c, rows, :].astype(BF)

    swap_d = remote(do, xr2, other_core)
    swap_d.start()
    second0 = reduce_second(0, first0)
    inputs_back(0)
    second1 = reduce_second(1, first1)
    third0 = reduce_third(0, second0)
    swap_d.wait()

    @pl.loop(0, 4)
    def _(part):
        rows = pl.ds(pl.multiple_of(part * 256, 256), 256)
        both = jnp.concatenate(
            [xh[0, c, rows, :].astype(BF) for c in range(3)] + [xr2[rows, :]], axis=1
        )
        dx_ref[0, rows, :] = nt(both, perm[...]).astype(BF)

    third1 = reduce_third(1, second1)
    reduce_last(0, third0)
    reduce_last(1, third1)
    for k in range(KW):
        wg_ref[k, :, 0:128] = fin[k * BLK : (k + 1) * BLK, :]

    def unplaced(lo, hi):
        value = fin[lo:hi, :]
        value = jnp.where(odd, swap(value), value)
        return value[:, :64], swap(value)[:, :64]

    for lo, k in ((240, 0), (288, 2)):
        one, two = unplaced(lo, lo + BLK)
        wg_ref[k, :, 128:192] = one
        wg_ref[k + 1, :, 128:192] = two
    one, two = unplaced(336, 368)
    wg_ref[4, 0:32, 128:192] = one
    wg_ref[4, 32:48, 128:192] = two[:16]


def on_device(inputs, trunk_grad, weights):
    vm = pltpu.VMEM
    scratch = [
        vm((1024, CIN), BF), vm((192, 4096), BF), vm((KW, BLK, 192), BF),
        vm((4096 + 2 * HALO, 192), BF), vm((8, EXT // 2, 128), BF),
        vm((2, EXT, COUT), BF), vm((8, EXT // 2, 128), BF),
        vm((CIN, CIN), BF), vm((CIN, HALF), BF),
        vm((2, 3, 1024, 128), F32), vm((1024, HALF), BF), vm((1024, HALF), BF),
        vm((1024, HALF), BF), vm((1024, HALF), BF),
        vm((CIN, 512), F32), vm((3, CIN, 1152), BF), vm((2, 3, 1024, 128), F32),
        vm((4, 4, 4, PIECE, 128), BF), vm((KW, HALF, COUT), BF),
        vm((4, 4, 4, PIECE, 128), BF), vm((4, TILE, HALF), F32), vm((PIECE, 128), F32),
    ]
    sizes = [size for group in REDUCE for _, size in group]
    scratch += [vm((3, 4, 4, n, 128), BF) for n in sizes]
    scratch += [vm((4, 4, n, 128), BF) for n in sizes]
    scratch += [vm((3, 4, n, 128), BF) for n in sizes]
    scratch += [vm((4, n, 128), F32) for n in sizes]
    scratch += [vm((3, n, 128), F32) for n in sizes]
    copies = 27 + 14 + 4 + 54
    scratch += [
        pltpu.SemaphoreType.DMA((3,)),
        pltpu.SemaphoreType.DMA((copies,)),
        pltpu.SemaphoreType.DMA((copies,)),
    ]
    return pl.pallas_call(
        kernel,
        out_shape=(
            jax.ShapeDtypeStruct((1, 1024, CIN), BF),
            jax.ShapeDtypeStruct((KW, BLK, 192), F32),
        ),
        in_specs=[pl.BlockSpec(memory_space=pl.ANY)] * 3,
        out_specs=(pl.BlockSpec(memory_space=pltpu.VMEM),) * 2,
        scratch_shapes=scratch,
        compiler_params=pltpu.CompilerParams(
            collective_id=0, has_side_effects=True, vmem_limit_bytes=63 * 1024 * 1024
        ),
        name="block_backward",
    )(inputs, jnp.swapaxes(trunk_grad, 1, 2), weights)


def solution(mesh):
    in_specs = (P("rep", "seq", None), P("rep", None, "seq"), P(None, "rep", "seq"))
    out_specs = (P("rep", "seq", None), P(None, "rep", "seq"))
    return jax.shard_map(
        on_device, mesh=mesh, in_specs=in_specs, out_specs=out_specs, check_vma=False
    )
```

```python
import functools

import jax
import jax.numpy as jnp
from jax import lax
from jax.experimental import pallas as pl
from jax.experimental.pallas import tpu as pltpu
from jax.sharding import PartitionSpec as P

MESH = pl.DeviceIdType.MESH
BF = jnp.bfloat16
F32 = jnp.float32

CIN, COUT, KW = 768, 1536, 5
HALF = CIN // 2
ROWS = 512
HALO = 16
EXT = ROWS + 2 * HALO
BLK = 48
PIECE = 368
GATHER = ((0, 160), (160, 96), (256, 112))
REDUCE = (((0, 80), (80, 80), (160, 80)), ((240, 48), (288, 48), (336, 32)))
RELAYED = (True, True)
TILE = 288


def nt(left, right):
    return lax.dot_general(
        left, right, (((1,), (1,)), ((), ())), preferred_element_type=F32
    )


def nn(left, right):
    return jnp.dot(left, right, preferred_element_type=F32)


def low_lanes(shape):
    return lax.broadcasted_iota(jnp.int32, shape, len(shape) - 1) < 64


def swap(value):
    return pltpu.roll(value, 64, 1)


def pack(direct, other):
    low = low_lanes(direct.shape)
    rolled = swap(other)
    return jnp.where(low, direct, rolled), jnp.where(low, rolled, direct)


def unpack(first, second):
    low = low_lanes(first.shape)
    return jnp.where(low, first, second), swap(jnp.where(low, second, first))


def channel_of(column, core):
    other = column >= HALF
    col = jnp.where(other, column - HALF, column)
    block = jnp.zeros_like(col)
    for t in range(1, 8):
        block = block + (col >= t * BLK).astype(jnp.int32)
    parity = jnp.where(other, 1 - core, core)
    return (2 * block + parity) * BLK + (col - block * BLK)


def kernel(
    x_hbm, g_hbm, w_hbm, dx_ref, wg_ref,
    xin, gin, win, gpad, stail, grad, tails, perm, sel,
    xh, xo, xr, xr2, do, et, eot, slope, wa, wfull, wg, prod, fin, *rest,
):
    def four(n):
        return [[rest[n * 6 + g * 3 + p] for p in range(3)] for g in range(2)]

    r1, s1, r2, s2, r3 = [four(n) for n in range(5)]
    lsem, ssem, rsem = rest[30:]
    s = lax.axis_index("seq")
    r = lax.axis_index("rep")
    x, yhi = lax.rem(s, 4), s // 4
    ylo, z, core = r // 8, lax.rem(r // 2, 4), lax.rem(r, 2)
    y = yhi * 2 + ylo
    odd = lax.rem(x, 2) == 1

    def dev(px, py, pz, pc):
        return ((py // 2) * 4 + px, (lax.rem(py, 2) * 4 + pz) * 2 + pc)

    def at(axis, d):
        c = {"x": x, "y": y, "z": z}
        c[axis] = lax.rem(c[axis] + d, 4)
        return dev(c["x"], c["y"], c["z"], core), c[axis]

    other_core = dev(x, y, z, 1 - core)

    load_x = pltpu.make_async_copy(x_hbm.at[0], xin, lsem.at[0])
    load_g = pltpu.make_async_copy(g_hbm.at[0], gin, lsem.at[1])
    load_w = pltpu.make_async_copy(w_hbm, win, lsem.at[2])
    load_w.start()
    load_g.start()
    load_x.start()

    barrier = pltpu.get_barrier_semaphore()
    friends = [at(axis, d)[0] for axis in "xyz" for d in (1, 2, 3)]
    friends += [dev(lax.rem(x + d, 4), lax.rem(y + 2, 4), z, core) for d in (1, 2, 3)]
    friends.append(other_core)
    for friend in friends:
        pl.semaphore_signal(barrier, inc=1, device_id=friend, device_id_type=MESH)

    count = [0]

    def remote(src, dst, device):
        i = count[0]
        count[0] += 1
        return pltpu.make_async_remote_copy(
            src_ref=src, dst_ref=dst, send_sem=ssem.at[i], recv_sem=rsem.at[i],
            device_id=device, device_id_type=MESH,
        )

    load_w.wait()
    mine = wa.at[x, y, z]

    def tail_of(tap):
        return win[tap, :, 128:192].astype(F32)

    def placed(first, second):
        both = jnp.concatenate([first, second], axis=1)
        return jnp.where(odd, swap(both), both).astype(BF)

    for tap in range(KW):
        mine[tap * BLK : (tap + 1) * BLK, :] = win[tap, :, :128]
    mine[240:288, :] = placed(tail_of(0), tail_of(1))
    mine[288:336, :] = placed(tail_of(2), tail_of(3))
    last = tail_of(4)
    mine[336:368, :] = placed(
        last[:32], jnp.concatenate([last[32:], jnp.zeros((16, 64), F32)], axis=0)
    )

    ga, gb, gc = [pl.ds(start, size) for start, size in GATHER]
    ahead = 1 - 2 * core

    def at_ahead(axis, n):
        return at(axis, n * ahead + 4)

    class Line:
        def __init__(self, axis, block):
            self.axis, self.block = axis, block
            self.onward, _ = at_ahead(axis, 1)
            back, self.before = at_ahead(axis, -1)
            own = block({"x": x, "y": y, "z": z}[axis])
            self.first = remote(own, own, self.onward)
            self.second = remote(own, own, back)
            self.first.start()
            self.second.start()

        def relay(self):
            self.first.wait_recv()
            block = self.block(self.before)
            self.third = remote(block, block, self.onward)
            self.third.start()

        def finish(self):
            self.first.wait_send()
            self.second.wait()
            self.third.wait()

    def relay(lines):
        for line in lines:
            line.relay()

    def finish(lines):
        for line in lines:
            line.finish()

    def spread(axis, block):
        copies = [remote(block, block, at(axis, d)[0]) for d in (1, 2, 3)]
        for c in copies:
            c.start()
        return copies

    def settle(copies):
        for c in copies:
            c.wait()

    load_g.wait()
    gpad[0:HALO, :] = jnp.zeros((HALO, 192), BF)
    gpad[HALO + 4096 : 2 * HALO + 4096, :] = jnp.zeros((HALO, 192), BF)

    @pl.loop(0, 8)
    def _(part):
        cols = pl.ds(pl.multiple_of(part * 512, 512), 512)
        gpad[pl.ds(pl.multiple_of(part * 512 + HALO, 16), 512), :] = gin[:, cols].T

    @pl.loop(0, 8)
    def _(part):
        def half(start):
            rows = pl.ds(pl.multiple_of(part * 512 + start, 16), EXT // 2)
            return gpad[rows, 128:192].astype(F32)

        stail[part] = placed(half(0), half(EXT // 2))

    my_lanes = pl.ds(pl.multiple_of(s * 128, 128), 128)
    grad[0, :, my_lanes] = gpad[pl.ds(pl.multiple_of(s * 512, 512), EXT), 0:128]
    tails[s] = stail[s]

    row_i = lax.broadcasted_iota(jnp.int32, (CIN, CIN), 0)
    col_i = lax.broadcasted_iota(jnp.int32, (CIN, CIN), 1)
    perm[...] = jnp.where(row_i == channel_of(col_i, core), 1.0, 0.0).astype(BF)

    pl.semaphore_wait(barrier, len(friends))


    gather1 = (
        spread("y", wa.at[x, y, z, ga])
        + spread("y", wa.at[x, y, z, gb])
        + spread("x", wa.at[x, y, z, gc])
    )

    def scatter(offsets):
        copies = []
        for dx_, dy in offsets:
            px, phi = lax.rem(x + dx_, 4), lax.rem(yhi + dy, 2)
            ps = phi * 4 + px
            target = dev(px, phi * 2 + ylo, z, core)
            rows = pl.ds(pl.multiple_of(ps * 512, 512), EXT)
            copies.append(remote(gpad.at[rows, 0:128], grad.at[0, :, my_lanes], target))
            copies.append(remote(stail.at[ps], tails.at[s], target))
        for c in copies:
            c.start()
        return copies

    scatter_g = scatter(((0, 1),))

    settle(gather1)
    gather2 = (
        spread("x", wa.at[x, :, z, ga])
        + spread("z", wa.at[x, :, z, gb])
        + spread("z", wa.at[:, y, z, gc])
    )

    scatter_g += scatter(((1, 1), (3, 1), (2, 1), (2, 0), (1, 0), (3, 0)))

    load_x.wait()

    @pl.loop(0, 4)
    def _(part):
        rows = pl.ds(pl.multiple_of(part * 256, 256), 256)
        ordered = nn(xin[rows, :], perm[...])
        for c in range(3):
            xh[0, c, rows, :] = ordered[:, c * 128 : (c + 1) * 128]
        xo[rows, :] = ordered[:, HALF:].astype(BF)

    swap_x = remote(xo, xr, other_core)
    swap_x.start()


    def activate(q, part):
        for phase in (0, 1):
            for c in range(3):
                v = xh[q, c, pl.ds(part * 256 + phase, 128, stride=2), :]
                sq = v * v
                u = 0.7978845608028654 * (v + 0.044715 * (sq * v))
                t = jnp.tanh(u)
                half = 0.5 * (1.0 + t)
                act = (v * half).astype(BF)
                deriv = half + 0.5 * v * (1.0 - t * t) * (
                    0.7978845608028654 * (1.0 + 3.0 * 0.044715 * sq)
                )
                rows = pl.ds(pl.multiple_of(q * 512 + part * 128, 128), 128)
                cols = pl.ds(pl.multiple_of(part * 128, 128), 128)
                lo = phase * HALF + c * 128
                et[lo : lo + 128, cols] = act.astype(F32).T
                slope[phase, c, rows, :] = deriv

    def shift(q):
        @pl.loop(0, 6)
        def _(n):
            rows = pl.ds(pl.multiple_of(n * 128, 128), 128)
            cols = slice(q * 512, (q + 1) * 512)
            lane = lax.broadcasted_iota(jnp.int32, (128, 512), 1)
            edge = lax.broadcasted_iota(jnp.int32, (128, 64), 1)
            v = et[rows, :]
            eot[1, rows, cols] = v.astype(BF)
            eot[0, rows, cols] = jnp.where(lane == 511, 0.0, pltpu.roll(v, 511, 1)).astype(BF)
            eot[2, rows, cols] = jnp.where(lane == 0, 0.0, pltpu.roll(v, 1, 1)).astype(BF)
            for j, here, column in ((0, q * 32 + 15, v[:, 0:1]), (2, q * 32 + 16, v[:, 511:512])):
                old = eot[j, rows, 1024:1088].astype(F32) if q else 0.0
                eot[j, rows, 1024:1088] = jnp.where(edge == here, column, old).astype(BF)

    @pl.loop(0, 2)
    def _(part):
        activate(0, part)

    settle(gather2[:3])
    gather3 = [Line("z", lambda c: wa.at[:, :, c, ga])]
    settle(gather2[3:])
    gather3 += [
        Line("x", lambda c: wa.at[c, :, :, gb]),
        Line("y", lambda c: wa.at[:, c, :, gc]),
    ]

    @pl.loop(2, 4)
    def _(part):
        activate(0, part)

    shift(0)

    swap_x.wait()

    @pl.loop(0, 4)
    def _(part):
        rows = pl.ds(pl.multiple_of(part * 256, 256), 256)
        for c in range(3):
            xh[1, c, rows, :] = xr[rows, c * 128 : (c + 1) * 128].astype(F32)

    @pl.loop(0, 4)
    def _(part):
        activate(1, part)

    shift(1)

    row_s = lax.broadcasted_iota(jnp.int32, (CIN, HALF), 0)
    col_s = lax.broadcasted_iota(jnp.int32, (CIN, HALF), 1)
    is_tail = row_s >= 512
    tail_s = (row_s - 512) // 64
    natural = jnp.where(
        is_tail,
        tail_s * 192 + 128 + (row_s - 512 - tail_s * 64),
        (row_s // 128) * 192 + lax.rem(row_s, 128),
    )
    sel[...] = jnp.where(natural == channel_of(col_s, core), 1.0, 0.0).astype(BF)

    for c in scatter_g:
        c.wait()
    swap_g = remote(grad.at[0, :, 0:1024], grad.at[1, :, 0:1024], other_core)
    swap_g.start()

    for m in range(4):
        lanes = slice(1024 + m * 128, 1152 + m * 128)
        top, bottom = unpack(tails[2 * m].astype(F32), tails[2 * m + 1].astype(F32))
        grad[0, 0 : EXT // 2, lanes] = top.astype(BF)
        grad[0, EXT // 2 : EXT, lanes] = bottom.astype(BF)
    swap_t = remote(grad.at[0, :, 1024:1536], grad.at[1, :, 1024:1536], other_core)
    swap_t.start()
    relay(gather3[:1])
    swap_g.wait()
    swap_t.wait()

    scale = 0.5 * float(16 * 8192) ** (-0.5)

    def grads(start):
        cols = pl.ds(pl.multiple_of(start, 128), 256)
        right = jnp.concatenate(
            [grad[q, HALO : HALO + ROWS, cols] for q in (0, 1)]
            + [grad[q, lo : lo + HALO, cols] for q in (0, 1) for lo in (0, HALO + ROWS)],
            axis=0,
        )
        sums = [
            nn(eot[0, :, :1088], right) * scale,
            nn(eot[1, :, :1024], right[:1024]) * scale,
            nn(eot[2, :, :1088], right) * scale,
        ]
        a = [v[:HALF] for v in sums]
        b = [v[HALF:] for v in sums]
        return (a[2] + b[2], a[1] + b[2], a[1] + b[1], a[0] + b[1], a[0] + b[0])

    def main_tile(n):
        taps = grads(n * 256)
        for half in (0, 1):
            px = lax.rem(n, 2) * 2 + half
            for b in range(8):
                target = wg.at[px, (n // 2) * 2 + b // 4, b % 4]
                for k in range(KW):
                    target[k * BLK : (k + 1) * BLK, :] = taps[k][
                        b * BLK : (b + 1) * BLK, half * 128 : (half + 1) * 128
                    ].astype(BF)

    @pl.loop(0, 3)
    def _(n):
        main_tile(n)

    relay(gather3[1:])
    main_tile(3)

    def send_sums(axis, source, slots):
        copies = []
        for d in (1, 2, 3):
            device, c = at(axis, d)
            copies.append(remote(source(c), slots.at[d - 1], device))
        for c in copies:
            c.start()
        return copies

    class Sum:
        def __init__(self, axis, block, slots, relayed):
            self.block, self.slots, self.relayed = block, slots, relayed
            self.own = {"x": x, "y": y, "z": z}[axis]
            if not relayed:
                self.copies = send_sums(axis, lambda c: wg.at[block(c)], slots)
                return
            self.onward, self.after = at_ahead(axis, 1)
            back, before = at_ahead(axis, -1)
            _, far = at_ahead(axis, 2)
            self.first = remote(wg.at[block(far)], slots.at[0], self.onward)
            self.second = remote(wg.at[block(before)], slots.at[1], back)
            self.first.start()
            self.second.start()

        def total(self, c, i, j, terms):
            lead = [i, j]
            block = self.block(c)
            place = tuple(lead.pop(0) if isinstance(n, slice) else n for n in block[:3])
            value = wg[place + block[3:]].astype(F32)
            for d in terms:
                value = value + self.slots[d, i, j].astype(F32)
            return value

        def owned(self, i, j):
            return self.total(self.own, i, j, (1, 2) if self.relayed else (0, 1, 2))

        def relay(self):
            if not self.relayed:
                return
            self.first.wait_recv()
            slots = self.slots

            @pl.loop(0, 4)
            def _(i):
                for j in range(4):
                    slots[0, i, j] = self.total(self.after, i, j, (0,)).astype(BF)

            self.third = remote(slots.at[0], slots.at[2], self.onward)
            self.third.start()

        def finish(self, out):
            if self.relayed:
                self.first.wait_send()
                self.second.wait()
                self.third.wait()
            else:
                settle(self.copies)

            @pl.loop(0, 4)
            def _(i):
                for j in range(4):
                    out[i, j] = self.owned(i, j).astype(BF)

    every = slice(None)

    def reduce_first(g):
        ra, rb, rc = [pl.ds(start, size) for start, size in REDUCE[g]]
        return [
            Sum("z", lambda c: (every, every, c, ra), r1[g][0], RELAYED[g]),
            Sum("x", lambda c: (c, every, every, rb), r1[g][1], RELAYED[g]),
            Sum("y", lambda c: (every, c, every, rc), r1[g][2], RELAYED[g]),
        ]

    def reduce_second(g, lines):
        copies = []
        for n, (line, out, slots) in enumerate(zip(lines, s1[g], r2[g])):
            line.finish(out)
            if n == 0:
                copies += send_sums("y", lambda c: out.at[:, c], slots)
            elif n == 1:
                copies += send_sums("z", lambda c: out.at[:, c], slots)
            else:
                copies += send_sums("x", lambda c: out.at[c], slots)
        return copies

    def reduce_third(g, lines, copies):
        settle(copies)
        (a2, b2, c2), (a3, b3, c3), (a4, b4, c4) = r2[g], s2[g], r3[g]
        add_up2(lambda i: lines[0].owned(i, y), a2, a3)
        add_up2(lambda i: lines[1].owned(i, z), b2, b3)
        add_up2(lambda i: lines[2].owned(x, i), c2, c3)
        return (
            send_sums("x", lambda c: a3.at[c], a4)
            + send_sums("y", lambda c: b3.at[c], b4)
            + send_sums("z", lambda c: c3.at[c], c4)
        )

    def reduce_last(g, copies):
        settle(copies)
        for (start, size), own, slots in zip(
            REDUCE[g], (s2[g][0][x], s2[g][1][y], s2[g][2][z]), r3[g]
        ):
            fin[start : start + size, :] = own + slots[0] + slots[1] + slots[2]

    def add_up2(own, slots, out):
        for i in range(4):
            total = own(i)
            for d in range(3):
                total = total + slots[d, i].astype(F32)
            out[i] = total

    first0 = reduce_first(0)

    @pl.loop(0, 2)
    def _(n):
        taps = grads(1024 + n * 256)
        for m in (0, 1):
            lanes = slice(m * 128, (m + 1) * 128)
            for b in range(8):
                rows = slice(b * BLK, (b + 1) * BLK)
                v = [tap[rows, lanes] for tap in taps]
                first = wg.at[m * 2, n * 2 + b // 4, b % 4]
                second = wg.at[m * 2 + 1, n * 2 + b // 4, b % 4]
                for lo, hi, one, two in (
                    (240, 288, v[0], v[1]),
                    (288, 336, v[2], v[3]),
                    (
                        336, 368, v[4][:32],
                        jnp.concatenate([v[4][32:], jnp.zeros((16, 128), F32)], axis=0),
                    ),
                ):
                    left, right = pack(one, two)
                    first[lo:hi, :] = left.astype(BF)
                    second[lo:hi, :] = right.astype(BF)

    first1 = reduce_first(1)

    finish(gather3)

    @pl.loop(0, 8)
    def _(b):
        bhi, blo = b // 4, lax.rem(b, 4)
        base = b * BLK
        rows = pl.ds(pl.multiple_of(base, 16), BLK)
        for t in range(8):
            source = wa.at[t % 4, (t // 4) * 2 + bhi, blo]
            for k in range(KW):
                wfull[k, rows, t * 128 : (t + 1) * 128] = source[k * BLK : (k + 1) * BLK, :]
        for m in range(4):
            lanes = slice(1024 + m * 128, 1152 + m * 128)
            first = wa.at[(2 * m) % 4, (m // 2) * 2 + bhi, blo]
            second = wa.at[(2 * m + 1) % 4, (m // 2) * 2 + bhi, blo]
            for lo, k in ((240, 0), (288, 2)):
                one, two = unpack(
                    first[lo : lo + BLK, :].astype(F32), second[lo : lo + BLK, :].astype(F32)
                )
                wfull[k, rows, lanes] = one.astype(BF)
                wfull[k + 1, rows, lanes] = two.astype(BF)
            one, two = unpack(first[336:368, :].astype(F32), second[336:368, :].astype(F32))
            wfull[4, pl.ds(pl.multiple_of(base, 16), 32), lanes] = one.astype(BF)
            wfull[4, pl.ds(pl.multiple_of(base + 32, 16), 16), lanes] = two[:16].astype(BF)

    def inputs_back(q):
        @pl.loop(0, 2)
        def _(part):
            block = grad[q, pl.ds(pl.multiple_of(part * 256, 256), TILE), :]
            for n, k in enumerate((0, 1, 3, 4)):
                prod[n] = nt(block, wfull[k])
            middle = block[HALO : HALO + 256]
            skip = nn(
                jnp.concatenate([middle[:, :512], middle[:, 1024:1280]], axis=1), sel[...]
            )
            shared = nt(middle, wfull[2])
            here = slice(HALO, HALO + 256)
            after = slice(HALO + 1, HALO + 257)
            before = slice(HALO - 1, HALO + 255)
            shared = shared + prod[0, after, :] + prod[3, before, :]
            even = shared + prod[1, here, :] + prod[2, before, :]
            odd_ = shared + prod[1, after, :] + prod[2, here, :]
            rows = pl.ds(pl.multiple_of(q * 512 + part * 256, 256), 256)
            for phase, value in ((0, even), (1, odd_)):
                for c in range(3):
                    lanes = slice(c * 128, (c + 1) * 128)
                    out = 0.5 * (value[:, lanes] * slope[phase, c, rows, :] + skip[:, lanes])
                    xh[q, c, pl.ds(part * 512 + phase, 256, stride=2), :] = out

    inputs_back(1)

    @pl.loop(0, 4)
    def _(part):
        rows = pl.ds(pl.multiple_of(part * 256, 256), 256)
        for c in range(3):
            do[rows, c * 128 : (c + 1) * 128] = xh[1, c, rows, :].astype(BF)

    swap_d = remote(do, xr2, other_core)
    swap_d.start()
    relay(first0)
    relay(first1)
    inputs_back(0)
    second0 = reduce_second(0, first0)
    second1 = reduce_second(1, first1)
    third0 = reduce_third(0, first0, second0)
    swap_d.wait()

    @pl.loop(0, 4)
    def _(part):
        rows = pl.ds(pl.multiple_of(part * 256, 256), 256)
        both = jnp.concatenate(
            [xh[0, c, rows, :].astype(BF) for c in range(3)] + [xr2[rows, :]], axis=1
        )
        dx_ref[0, rows, :] = nt(both, perm[...]).astype(BF)

    third1 = reduce_third(1, first1, second1)
    reduce_last(0, third0)
    reduce_last(1, third1)
    for k in range(KW):
        wg_ref[k, :, 0:128] = fin[k * BLK : (k + 1) * BLK, :]

    def unplaced(lo, hi):
        value = fin[lo:hi, :]
        value = jnp.where(odd, swap(value), value)
        return value[:, :64], swap(value)[:, :64]

    for lo, k in ((240, 0), (288, 2)):
        one, two = unplaced(lo, lo + BLK)
        wg_ref[k, :, 128:192] = one
        wg_ref[k + 1, :, 128:192] = two
    one, two = unplaced(336, 368)
    wg_ref[4, 0:32, 128:192] = one
    wg_ref[4, 32:48, 128:192] = two[:16]


def on_device(inputs, trunk_grad, weights):
    vm = pltpu.VMEM
    scratch = [
        vm((1024, CIN), BF), vm((192, 4096), BF), vm((KW, BLK, 192), BF),
        vm((4096 + 2 * HALO, 192), BF), vm((8, EXT // 2, 128), BF),
        vm((2, EXT, COUT), BF), vm((8, EXT // 2, 128), BF),
        vm((CIN, CIN), BF), vm((CIN, HALF), BF),
        vm((2, 3, 1024, 128), F32), vm((1024, HALF), BF), vm((1024, HALF), BF),
        vm((1024, HALF), BF), vm((1024, HALF), BF),
        vm((CIN, 512), F32), vm((3, CIN, 1152), BF), vm((2, 3, 1024, 128), F32),
        vm((4, 4, 4, PIECE, 128), BF), vm((KW, HALF, COUT), BF),
        vm((4, 4, 4, PIECE, 128), BF), vm((4, TILE, HALF), F32), vm((PIECE, 128), F32),
    ]
    sizes = [size for group in REDUCE for _, size in group]
    scratch += [vm((3, 4, 4, n, 128), BF) for n in sizes]
    scratch += [vm((4, 4, n, 128), BF) for n in sizes]
    scratch += [vm((3, 4, n, 128), BF) for n in sizes]
    scratch += [vm((4, n, 128), F32) for n in sizes]
    scratch += [vm((3, n, 128), F32) for n in sizes]
    copies = 27 + 14 + 4 + 54
    scratch += [
        pltpu.SemaphoreType.DMA((3,)),
        pltpu.SemaphoreType.DMA((copies,)),
        pltpu.SemaphoreType.DMA((copies,)),
    ]
    return pl.pallas_call(
        kernel,
        out_shape=(
            jax.ShapeDtypeStruct((1, 1024, CIN), BF),
            jax.ShapeDtypeStruct((KW, BLK, 192), F32),
        ),
        in_specs=[pl.BlockSpec(memory_space=pl.ANY)] * 3,
        out_specs=(pl.BlockSpec(memory_space=pltpu.VMEM),) * 2,
        scratch_shapes=scratch,
        compiler_params=pltpu.CompilerParams(
            collective_id=0, has_side_effects=True, vmem_limit_bytes=63 * 1024 * 1024
        ),
        name="block_backward",
    )(inputs, jnp.swapaxes(trunk_grad, 1, 2), weights)


def solution(mesh):
    in_specs = (P("rep", "seq", None), P("rep", None, "seq"), P(None, "rep", "seq"))
    out_specs = (P("rep", "seq", None), P(None, "rep", "seq"))
    return jax.shard_map(
        on_device, mesh=mesh, in_specs=in_specs, out_specs=out_specs, check_vma=False
    )
```

```python
import functools

import jax
import jax.numpy as jnp
from jax import lax
from jax.experimental import pallas as pl
from jax.experimental.pallas import tpu as pltpu
from jax.sharding import PartitionSpec as P

MESH = pl.DeviceIdType.MESH
BF = jnp.bfloat16
F32 = jnp.float32

CIN, COUT, KW = 768, 1536, 5
HALF = CIN // 2
ROWS = 512
HALO = 16
EXT = ROWS + 2 * HALO
BLK = 48
PIECE = 368
GATHER = ((0, 160), (160, 96), (256, 112))
REDUCE = (((0, 80), (80, 80), (160, 80)), ((240, 48), (288, 48), (336, 32)))
RELAYED = (True, True)


def nt(left, right):
    return lax.dot_general(
        left, right, (((1,), (1,)), ((), ())), preferred_element_type=F32
    )


def nn(left, right):
    return jnp.dot(left, right, preferred_element_type=F32)


def low_lanes(shape):
    return lax.broadcasted_iota(jnp.int32, shape, len(shape) - 1) < 64


def swap(value):
    return pltpu.roll(value, 64, 1)


def pack(direct, other):
    low = low_lanes(direct.shape)
    rolled = swap(other)
    return jnp.where(low, direct, rolled), jnp.where(low, rolled, direct)


def unpack(first, second):
    low = low_lanes(first.shape)
    return jnp.where(low, first, second), swap(jnp.where(low, second, first))


def channel_of(column, core):
    other = column >= HALF
    col = jnp.where(other, column - HALF, column)
    block = jnp.zeros_like(col)
    for t in range(1, 8):
        block = block + (col >= t * BLK).astype(jnp.int32)
    parity = jnp.where(other, 1 - core, core)
    return (2 * block + parity) * BLK + (col - block * BLK)


def kernel(
    x_hbm, g_hbm, w_hbm, dx_ref, wg_ref,
    xin, gin, win, gpad, stail, grad, tails, perm, sel,
    xh, xo, xr, xr2, do, et, eot, slope, wa, wfull, wg, prod, fin, *rest,
):
    def four(n):
        return [[rest[n * 6 + g * 3 + p] for p in range(3)] for g in range(2)]

    r1, s1, r2, s2, r3 = [four(n) for n in range(5)]
    lsem, ssem, rsem = rest[30:]
    s = lax.axis_index("seq")
    r = lax.axis_index("rep")
    x, yhi = lax.rem(s, 4), s // 4
    ylo, z, core = r // 8, lax.rem(r // 2, 4), lax.rem(r, 2)
    y = yhi * 2 + ylo
    odd = lax.rem(x, 2) == 1

    def dev(px, py, pz, pc):
        return ((py // 2) * 4 + px, (lax.rem(py, 2) * 4 + pz) * 2 + pc)

    def at(axis, d):
        c = {"x": x, "y": y, "z": z}
        c[axis] = lax.rem(c[axis] + d, 4)
        return dev(c["x"], c["y"], c["z"], core), c[axis]

    other_core = dev(x, y, z, 1 - core)

    load_x = pltpu.make_async_copy(x_hbm.at[0], xin, lsem.at[0])
    load_g = pltpu.make_async_copy(g_hbm.at[0], gin, lsem.at[1])
    load_w = pltpu.make_async_copy(w_hbm, win, lsem.at[2])
    load_w.start()
    load_g.start()
    load_x.start()

    barrier = pltpu.get_barrier_semaphore()
    friends = [at(axis, d)[0] for axis in "xyz" for d in (1, 2, 3)]
    friends += [dev(lax.rem(x + d, 4), lax.rem(y + 2, 4), z, core) for d in (1, 2, 3)]
    friends.append(other_core)
    for friend in friends:
        pl.semaphore_signal(barrier, inc=1, device_id=friend, device_id_type=MESH)

    count = [0]

    def remote(src, dst, device):
        i = count[0]
        count[0] += 1
        return pltpu.make_async_remote_copy(
            src_ref=src, dst_ref=dst, send_sem=ssem.at[i], recv_sem=rsem.at[i],
            device_id=device, device_id_type=MESH,
        )

    load_w.wait()
    mine = wa.at[x, y, z]

    def tail_of(tap):
        return win[tap, :, 128:192].astype(F32)

    def placed(first, second):
        both = jnp.concatenate([first, second], axis=1)
        return jnp.where(odd, swap(both), both).astype(BF)

    for tap in range(KW):
        mine[tap * BLK : (tap + 1) * BLK, :] = win[tap, :, :128]
    mine[240:288, :] = placed(tail_of(0), tail_of(1))
    mine[288:336, :] = placed(tail_of(2), tail_of(3))
    last = tail_of(4)
    mine[336:368, :] = placed(
        last[:32], jnp.concatenate([last[32:], jnp.zeros((16, 64), F32)], axis=0)
    )

    ga, gb, gc = [pl.ds(start, size) for start, size in GATHER]
    ahead = 1 - 2 * core

    def at_ahead(axis, n):
        return at(axis, n * ahead + 4)

    class Line:
        def __init__(self, axis, block):
            self.axis, self.block = axis, block
            self.onward, _ = at_ahead(axis, 1)
            back, self.before = at_ahead(axis, -1)
            own = block({"x": x, "y": y, "z": z}[axis])
            self.first = remote(own, own, self.onward)
            self.second = remote(own, own, back)
            self.first.start()
            self.second.start()

        def relay(self):
            self.first.wait_recv()
            block = self.block(self.before)
            self.third = remote(block, block, self.onward)
            self.third.start()

        def finish(self):
            self.first.wait_send()
            self.second.wait()
            self.third.wait()

    def relay(lines):
        for line in lines:
            line.relay()

    def finish(lines):
        for line in lines:
            line.finish()

    def spread(axis, block):
        copies = [remote(block, block, at(axis, d)[0]) for d in (1, 2, 3)]
        for c in copies:
            c.start()
        return copies

    def settle(copies):
        for c in copies:
            c.wait()

    load_g.wait()
    gpad[0:HALO, :] = jnp.zeros((HALO, 192), BF)
    gpad[HALO + 4096 : 2 * HALO + 4096, :] = jnp.zeros((HALO, 192), BF)

    @pl.loop(0, 8)
    def _(part):
        cols = pl.ds(pl.multiple_of(part * 512, 512), 512)
        gpad[pl.ds(pl.multiple_of(part * 512 + HALO, 16), 512), :] = gin[:, cols].T

    @pl.loop(0, 8)
    def _(part):
        def half(start):
            rows = pl.ds(pl.multiple_of(part * 512 + start, 16), EXT // 2)
            return gpad[rows, 128:192].astype(F32)

        stail[part] = placed(half(0), half(EXT // 2))

    my_lanes = pl.ds(pl.multiple_of(s * 128, 128), 128)
    grad[0, :, my_lanes] = gpad[pl.ds(pl.multiple_of(s * 512, 512), EXT), 0:128]
    tails[s] = stail[s]

    row_i = lax.broadcasted_iota(jnp.int32, (CIN, CIN), 0)
    col_i = lax.broadcasted_iota(jnp.int32, (CIN, CIN), 1)
    perm[...] = jnp.where(row_i == channel_of(col_i, core), 1.0, 0.0).astype(BF)

    pl.semaphore_wait(barrier, len(friends))


    gather1 = (
        spread("y", wa.at[x, y, z, ga])
        + spread("y", wa.at[x, y, z, gb])
        + spread("x", wa.at[x, y, z, gc])
    )

    def scatter(offsets):
        copies = []
        for dx_, dy in offsets:
            px, phi = lax.rem(x + dx_, 4), lax.rem(yhi + dy, 2)
            ps = phi * 4 + px
            target = dev(px, phi * 2 + ylo, z, core)
            rows = pl.ds(pl.multiple_of(ps * 512, 512), EXT)
            copies.append(remote(gpad.at[rows, 0:128], grad.at[0, :, my_lanes], target))
            copies.append(remote(stail.at[ps], tails.at[s], target))
        for c in copies:
            c.start()
        return copies

    scatter_g = scatter(((0, 1),))

    settle(gather1)
    gather2 = (
        spread("x", wa.at[x, :, z, ga])
        + spread("z", wa.at[x, :, z, gb])
        + spread("z", wa.at[:, y, z, gc])
    )

    scatter_g += scatter(((1, 1), (3, 1), (2, 1), (2, 0), (1, 0), (3, 0)))

    load_x.wait()

    @pl.loop(0, 4)
    def _(part):
        rows = pl.ds(pl.multiple_of(part * 256, 256), 256)
        ordered = nn(xin[rows, :], perm[...])
        for c in range(3):
            xh[0, c, rows, :] = ordered[:, c * 128 : (c + 1) * 128]
        xo[rows, :] = ordered[:, HALF:].astype(BF)

    swap_x = remote(xo, xr, other_core)
    swap_x.start()


    def activate(q, part):
        for phase in (0, 1):
            for c in range(3):
                v = xh[q, c, pl.ds(part * 256 + phase, 128, stride=2), :]
                sq = v * v
                u = 0.7978845608028654 * (v + 0.044715 * (sq * v))
                t = jnp.tanh(u)
                half = 0.5 * (1.0 + t)
                act = (v * half).astype(BF)
                deriv = half + 0.5 * v * (1.0 - t * t) * (
                    0.7978845608028654 * (1.0 + 3.0 * 0.044715 * sq)
                )
                rows = pl.ds(pl.multiple_of(q * 512 + part * 128, 128), 128)
                cols = pl.ds(pl.multiple_of(part * 128, 128), 128)
                lo = phase * HALF + c * 128
                et[lo : lo + 128, cols] = act.astype(F32).T
                slope[phase, c, rows, :] = deriv

    def shift(q):
        @pl.loop(0, 6)
        def _(n):
            rows = pl.ds(pl.multiple_of(n * 128, 128), 128)
            cols = slice(q * 512, (q + 1) * 512)
            lane = lax.broadcasted_iota(jnp.int32, (128, 512), 1)
            edge = lax.broadcasted_iota(jnp.int32, (128, 64), 1)
            v = et[rows, :]
            eot[1, rows, cols] = v.astype(BF)
            eot[0, rows, cols] = jnp.where(lane == 511, 0.0, pltpu.roll(v, 511, 1)).astype(BF)
            eot[2, rows, cols] = jnp.where(lane == 0, 0.0, pltpu.roll(v, 1, 1)).astype(BF)
            for j, here, column in ((0, q * 32 + 15, v[:, 0:1]), (2, q * 32 + 16, v[:, 511:512])):
                old = eot[j, rows, 1024:1088].astype(F32) if q else 0.0
                eot[j, rows, 1024:1088] = jnp.where(edge == here, column, old).astype(BF)

    @pl.loop(0, 2)
    def _(part):
        activate(0, part)

    settle(gather2[:3])
    gather3 = [Line("z", lambda c: wa.at[:, :, c, ga])]
    settle(gather2[3:])
    gather3 += [
        Line("x", lambda c: wa.at[c, :, :, gb]),
        Line("y", lambda c: wa.at[:, c, :, gc]),
    ]

    @pl.loop(2, 4)
    def _(part):
        activate(0, part)

    shift(0)

    swap_x.wait()

    @pl.loop(0, 4)
    def _(part):
        rows = pl.ds(pl.multiple_of(part * 256, 256), 256)
        for c in range(3):
            xh[1, c, rows, :] = xr[rows, c * 128 : (c + 1) * 128].astype(F32)

    @pl.loop(0, 4)
    def _(part):
        activate(1, part)

    shift(1)

    row_s = lax.broadcasted_iota(jnp.int32, (CIN, HALF), 0)
    col_s = lax.broadcasted_iota(jnp.int32, (CIN, HALF), 1)
    is_tail = row_s >= 512
    tail_s = (row_s - 512) // 64
    natural = jnp.where(
        is_tail,
        tail_s * 192 + 128 + (row_s - 512 - tail_s * 64),
        (row_s // 128) * 192 + lax.rem(row_s, 128),
    )
    sel[...] = jnp.where(natural == channel_of(col_s, core), 1.0, 0.0).astype(BF)

    for c in scatter_g:
        c.wait()
    swap_g = remote(grad.at[0, :, 0:1024], grad.at[1, :, 0:1024], other_core)
    swap_g.start()

    for m in range(4):
        lanes = slice(1024 + m * 128, 1152 + m * 128)
        top, bottom = unpack(tails[2 * m].astype(F32), tails[2 * m + 1].astype(F32))
        grad[0, 0 : EXT // 2, lanes] = top.astype(BF)
        grad[0, EXT // 2 : EXT, lanes] = bottom.astype(BF)
    swap_t = remote(grad.at[0, :, 1024:1536], grad.at[1, :, 1024:1536], other_core)
    swap_t.start()
    relay(gather3[:1])
    swap_g.wait()
    swap_t.wait()

    scale = 0.5 * float(16 * 8192) ** (-0.5)

    def grads(start):
        cols = pl.ds(pl.multiple_of(start, 128), 256)
        right = jnp.concatenate(
            [grad[q, HALO : HALO + ROWS, cols] for q in (0, 1)]
            + [grad[q, lo : lo + HALO, cols] for q in (0, 1) for lo in (0, HALO + ROWS)],
            axis=0,
        )
        sums = [
            nn(eot[0, :, :1088], right) * scale,
            nn(eot[1, :, :1024], right[:1024]) * scale,
            nn(eot[2, :, :1088], right) * scale,
        ]
        a = [v[:HALF] for v in sums]
        b = [v[HALF:] for v in sums]
        return (a[2] + b[2], a[1] + b[2], a[1] + b[1], a[0] + b[1], a[0] + b[0])

    def main_tile(n):
        taps = grads(n * 256)
        for half in (0, 1):
            px = lax.rem(n, 2) * 2 + half
            for b in range(8):
                target = wg.at[px, (n // 2) * 2 + b // 4, b % 4]
                for k in range(KW):
                    target[k * BLK : (k + 1) * BLK, :] = taps[k][
                        b * BLK : (b + 1) * BLK, half * 128 : (half + 1) * 128
                    ].astype(BF)

    @pl.loop(0, 1)
    def _(n):
        main_tile(n)

    relay(gather3[1:])

    @pl.loop(1, 4)
    def _(n):
        main_tile(n)


    def send_sums(axis, source, slots):
        copies = []
        for d in (1, 2, 3):
            device, c = at(axis, d)
            copies.append(remote(source(c), slots.at[d - 1], device))
        for c in copies:
            c.start()
        return copies

    class Sum:
        def __init__(self, axis, block, slots, relayed):
            self.block, self.slots, self.relayed = block, slots, relayed
            self.own = {"x": x, "y": y, "z": z}[axis]
            if not relayed:
                self.copies = send_sums(axis, lambda c: wg.at[block(c)], slots)
                return
            self.onward, self.after = at_ahead(axis, 1)
            back, before = at_ahead(axis, -1)
            _, far = at_ahead(axis, 2)
            self.first = remote(wg.at[block(far)], slots.at[0], self.onward)
            self.second = remote(wg.at[block(before)], slots.at[1], back)
            self.first.start()
            self.second.start()

        def total(self, c, i, j, terms):
            lead = [i, j]
            block = self.block(c)
            place = tuple(lead.pop(0) if isinstance(n, slice) else n for n in block[:3])
            value = wg[place + block[3:]].astype(F32)
            for d in terms:
                value = value + self.slots[d, i, j].astype(F32)
            return value

        def owned(self, i, j):
            return self.total(self.own, i, j, (1, 2) if self.relayed else (0, 1, 2))

        def relay(self):
            if not self.relayed:
                return
            self.first.wait_recv()
            slots = self.slots

            @pl.loop(0, 4)
            def _(i):
                for j in range(4):
                    slots[0, i, j] = self.total(self.after, i, j, (0,)).astype(BF)

            self.third = remote(slots.at[0], slots.at[2], self.onward)
            self.third.start()

        def finish(self, out):
            if self.relayed:
                self.first.wait_send()
                self.second.wait()
                self.third.wait()
            else:
                settle(self.copies)

            @pl.loop(0, 4)
            def _(i):
                for j in range(4):
                    out[i, j] = self.owned(i, j).astype(BF)

    every = slice(None)

    def reduce_first(g):
        ra, rb, rc = [pl.ds(start, size) for start, size in REDUCE[g]]
        return [
            Sum("z", lambda c: (every, every, c, ra), r1[g][0], RELAYED[g]),
            Sum("x", lambda c: (c, every, every, rb), r1[g][1], RELAYED[g]),
            Sum("y", lambda c: (every, c, every, rc), r1[g][2], RELAYED[g]),
        ]

    def reduce_second(g, lines):
        copies = []
        for n, (line, out, slots) in enumerate(zip(lines, s1[g], r2[g])):
            line.finish(out)
            if n == 0:
                copies += send_sums("y", lambda c: out.at[:, c], slots)
            elif n == 1:
                copies += send_sums("z", lambda c: out.at[:, c], slots)
            else:
                copies += send_sums("x", lambda c: out.at[c], slots)
        return copies

    def reduce_third(g, lines, copies):
        settle(copies)
        (a2, b2, c2), (a3, b3, c3), (a4, b4, c4) = r2[g], s2[g], r3[g]
        add_up2(lambda i: lines[0].owned(i, y), a2, a3)
        add_up2(lambda i: lines[1].owned(i, z), b2, b3)
        add_up2(lambda i: lines[2].owned(x, i), c2, c3)
        return (
            send_sums("x", lambda c: a3.at[c], a4)
            + send_sums("y", lambda c: b3.at[c], b4)
            + send_sums("z", lambda c: c3.at[c], c4)
        )

    def reduce_last(g, copies):
        settle(copies)
        for (start, size), own, slots in zip(
            REDUCE[g], (s2[g][0][x], s2[g][1][y], s2[g][2][z]), r3[g]
        ):
            fin[start : start + size, :] = own + slots[0] + slots[1] + slots[2]

    def add_up2(own, slots, out):
        for i in range(4):
            total = own(i)
            for d in range(3):
                total = total + slots[d, i].astype(F32)
            out[i] = total

    first0 = reduce_first(0)

    @pl.loop(0, 2)
    def _(n):
        taps = grads(1024 + n * 256)
        for m in (0, 1):
            lanes = slice(m * 128, (m + 1) * 128)
            for b in range(8):
                rows = slice(b * BLK, (b + 1) * BLK)
                v = [tap[rows, lanes] for tap in taps]
                first = wg.at[m * 2, n * 2 + b // 4, b % 4]
                second = wg.at[m * 2 + 1, n * 2 + b // 4, b % 4]
                for lo, hi, one, two in (
                    (240, 288, v[0], v[1]),
                    (288, 336, v[2], v[3]),
                    (
                        336, 368, v[4][:32],
                        jnp.concatenate([v[4][32:], jnp.zeros((16, 128), F32)], axis=0),
                    ),
                ):
                    left, right = pack(one, two)
                    first[lo:hi, :] = left.astype(BF)
                    second[lo:hi, :] = right.astype(BF)

    first1 = reduce_first(1)

    finish(gather3)

    @pl.loop(0, 8)
    def _(b):
        bhi, blo = b // 4, lax.rem(b, 4)
        base = b * BLK
        rows = pl.ds(pl.multiple_of(base, 16), BLK)
        for t in range(8):
            source = wa.at[t % 4, (t // 4) * 2 + bhi, blo]
            for k in range(KW):
                wfull[k, rows, t * 128 : (t + 1) * 128] = source[k * BLK : (k + 1) * BLK, :]
        for m in range(4):
            lanes = slice(1024 + m * 128, 1152 + m * 128)
            first = wa.at[(2 * m) % 4, (m // 2) * 2 + bhi, blo]
            second = wa.at[(2 * m + 1) % 4, (m // 2) * 2 + bhi, blo]
            for lo, k in ((240, 0), (288, 2)):
                one, two = unpack(
                    first[lo : lo + BLK, :].astype(F32), second[lo : lo + BLK, :].astype(F32)
                )
                wfull[k, rows, lanes] = one.astype(BF)
                wfull[k + 1, rows, lanes] = two.astype(BF)
            one, two = unpack(first[336:368, :].astype(F32), second[336:368, :].astype(F32))
            wfull[4, pl.ds(pl.multiple_of(base, 16), 32), lanes] = one.astype(BF)
            wfull[4, pl.ds(pl.multiple_of(base + 32, 16), 16), lanes] = two[:16].astype(BF)

    def inputs_back(q):
        for n, k in enumerate((0, 1, 3, 4, 2)):
            prod[n] = nt(grad[q], wfull[k])

        for part in (0, 1):
            rows = pl.ds(pl.multiple_of(q * 512 + part * 256, 256), 256)
            middle = grad[q, pl.ds(pl.multiple_of(part * 256 + HALO, 16), 256), :]
            skip = nn(
                jnp.concatenate([middle[:, :512], middle[:, 1024:1280]], axis=1), sel[...]
            )

            def shifted(n, by, part=part):
                start = part * 256 + HALO + by
                return prod[n, start : start + 256, :]

            shared = shifted(4, 0) + shifted(0, 1) + shifted(3, -1)
            even = shared + shifted(1, 0) + shifted(2, -1)
            odd_ = shared + shifted(1, 1) + shifted(2, 0)
            for phase, value in ((0, even), (1, odd_)):
                for c in range(3):
                    lanes = slice(c * 128, (c + 1) * 128)
                    out = 0.5 * (value[:, lanes] * slope[phase, c, rows, :] + skip[:, lanes])
                    xh[q, c, pl.ds(part * 512 + phase, 256, stride=2), :] = out

    inputs_back(1)

    @pl.loop(0, 4)
    def _(part):
        rows = pl.ds(pl.multiple_of(part * 256, 256), 256)
        for c in range(3):
            do[rows, c * 128 : (c + 1) * 128] = xh[1, c, rows, :].astype(BF)

    swap_d = remote(do, xr2, other_core)
    swap_d.start()
    relay(first0)
    relay(first1)
    inputs_back(0)
    second0 = reduce_second(0, first0)
    second1 = reduce_second(1, first1)
    third0 = reduce_third(0, first0, second0)
    swap_d.wait()

    @pl.loop(0, 4)
    def _(part):
        rows = pl.ds(pl.multiple_of(part * 256, 256), 256)
        both = jnp.concatenate(
            [xh[0, c, rows, :].astype(BF) for c in range(3)] + [xr2[rows, :]], axis=1
        )
        dx_ref[0, rows, :] = nt(both, perm[...]).astype(BF)

    third1 = reduce_third(1, first1, second1)
    reduce_last(0, third0)
    reduce_last(1, third1)
    for k in range(KW):
        wg_ref[k, :, 0:128] = fin[k * BLK : (k + 1) * BLK, :]

    def unplaced(lo, hi):
        value = fin[lo:hi, :]
        value = jnp.where(odd, swap(value), value)
        return value[:, :64], swap(value)[:, :64]

    for lo, k in ((240, 0), (288, 2)):
        one, two = unplaced(lo, lo + BLK)
        wg_ref[k, :, 128:192] = one
        wg_ref[k + 1, :, 128:192] = two
    one, two = unplaced(336, 368)
    wg_ref[4, 0:32, 128:192] = one
    wg_ref[4, 32:48, 128:192] = two[:16]


def on_device(inputs, trunk_grad, weights):
    vm = pltpu.VMEM
    scratch = [
        vm((1024, CIN), BF), vm((192, 4096), BF), vm((KW, BLK, 192), BF),
        vm((4096 + 2 * HALO, 192), BF), vm((8, EXT // 2, 128), BF),
        vm((2, EXT, COUT), BF), vm((8, EXT // 2, 128), BF),
        vm((CIN, CIN), BF), vm((CIN, HALF), BF),
        vm((2, 3, 1024, 128), F32), vm((1024, HALF), BF), vm((1024, HALF), BF),
        vm((1024, HALF), BF), vm((1024, HALF), BF),
        vm((CIN, 512), F32), vm((3, CIN, 1152), BF), vm((2, 3, 1024, 128), F32),
        vm((4, 4, 4, PIECE, 128), BF), vm((KW, HALF, COUT), BF),
        vm((4, 4, 4, PIECE, 128), BF), vm((5, EXT, HALF), F32), vm((PIECE, 128), F32),
    ]
    sizes = [size for group in REDUCE for _, size in group]
    scratch += [vm((3, 4, 4, n, 128), BF) for n in sizes]
    scratch += [vm((4, 4, n, 128), BF) for n in sizes]
    scratch += [vm((3, 4, n, 128), BF) for n in sizes]
    scratch += [vm((4, n, 128), F32) for n in sizes]
    scratch += [vm((3, n, 128), F32) for n in sizes]
    copies = 27 + 14 + 4 + 54
    scratch += [
        pltpu.SemaphoreType.DMA((3,)),
        pltpu.SemaphoreType.DMA((copies,)),
        pltpu.SemaphoreType.DMA((copies,)),
    ]
    return pl.pallas_call(
        kernel,
        out_shape=(
            jax.ShapeDtypeStruct((1, 1024, CIN), BF),
            jax.ShapeDtypeStruct((KW, BLK, 192), F32),
        ),
        in_specs=[pl.BlockSpec(memory_space=pl.ANY)] * 3,
        out_specs=(pl.BlockSpec(memory_space=pltpu.VMEM),) * 2,
        scratch_shapes=scratch,
        compiler_params=pltpu.CompilerParams(
            collective_id=0, has_side_effects=True, vmem_limit_bytes=63 * 1024 * 1024
        ),
        name="block_backward",
    )(inputs, jnp.swapaxes(trunk_grad, 1, 2), weights)


def solution(mesh):
    in_specs = (P("rep", "seq", None), P("rep", None, "seq"), P(None, "rep", "seq"))
    out_specs = (P("rep", "seq", None), P(None, "rep", "seq"))
    return jax.shard_map(
        on_device, mesh=mesh, in_specs=in_specs, out_specs=out_specs, check_vma=False
    )
```
